32 devices in a mesh: gy: 4 (over y, core), gx: 8 (over z, x).
Axes of the slice: x: 2, y: 2, z: 4, core: 2. Of those that a mesh axis runs over, the one named last changes fastest.
Arguments:
- ocean_blocks: float32 [256, 4, 1024], P('gy', None, 'gx'), may hold values from -4 to 4
- block_map: int32 [256, 8], P('gy', 'gx'), may hold values from 0 to 511, as said below
- velocity: float32 [2, 256, 1024], P(None, 'gy', 'gx'), may hold values from -2 to 2
- stress: float32 [3, 256, 1024], P(None, 'gy', 'gx'), may hold values from -3 to 3
- thickness: float32 [5, 256, 1024], P(None, 'gy', 'gx'), may hold values from 0.05 to 5
- area: float32 [5, 256, 1024], P(None, 'gy', 'gx'), may hold values from 0.1 to 0.2
- wind: float32 [2, 256, 1024], P(None, 'gy', 'gx'), may hold values from -3 to 3
- air_temp: float32 [256, 1024], P('gy', 'gx'), may hold values from -6 to 0
- ice_presence_mask: int32 [256, 1024], P('gy', 'gx'), may hold values 0 or 1
- ocean_land_mask: int32 [256, 1024], P('gy', 'gx'), may hold values 0 or 1
- fold_partner_column: int32 [1024], replicated, may hold values from 0 to 1023, as said below
Outputs:
- velocity_out: float32 [2, 256, 1024], P(None, 'gy', 'gx')
- stress_out: float32 [3, 256, 1024], P(None, 'gy', 'gx')
- thickness_out: float32 [5, 256, 1024], P(None, 'gy', 'gx')
The draws below stay inside these ranges and needn't reach their ends.
Inputs may be any that keep to these rules, and one draw needn't show every extreme that they name: Within each latitude row of devices block_map is a permutation of 0 to 511; value p * 64 + t names device p, row t. The slots k * 8 to (k + 1) * 8 - 1 of one device all go to one device, into rows k * 8 to (k + 1) * 8 - 1; different k of one device go to different devices. fold_partner_column[i] = (c - i) mod 1024 for one c per draw, so the table is its own inverse.
All inputs are finite; a program needn't handle non-finite values. No bound on the sum of `ice_presence_mask` or of `ocean_land_mask` on one device may be relied on, other than what follows from the above.
Results may differ from the reference program's by a relative error of at most 0.0001.
Values sent between devices are 32-bit elements; how exact they have to be, the bound alone decides.
A program may use at most 64 MiB of HBM per device.

```python
import math
import jax
import jax.numpy as jnp
from jax import lax

CY = 64
CX = 128
NCAT = 5
ITERS = 4
NY = 256
NX = 1024
N_GY = 4
N_GX = 8


def draw_block_map(key, part):
    group = max(2, CY // N_GX)
    count = CY // group

    def one_row(row_key):
        key_order, key_shift, key_inner = jax.random.split(row_key, 3)
        order = jax.random.permutation(key_order, N_GX).astype(jnp.int32)
        place = jnp.zeros((N_GX,), jnp.int32).at[order].set(jnp.arange(N_GX, dtype=jnp.int32))
        shifts = jax.random.permutation(key_shift, N_GX).astype(jnp.int32)[:count]
        inner_keys = jax.random.split(key_inner, N_GX * count)

        def inner_order(small_key):
            return jax.random.permutation(small_key, group).astype(jnp.int32)
        inner = jax.vmap(inner_order)(inner_keys).reshape(N_GX, count, group)
        dest_dev = order[(place[:, None] + shifts[None, :]) % N_GX]
        dest_row = jnp.arange(count, dtype=jnp.int32)[None, :, None] * group + inner
        value = dest_dev[:, :, None] * CY + dest_row
        return value.reshape(N_GX, CY).T
    row_keys = jax.random.split(jax.random.fold_in(key, 11), N_GY)
    rows = jax.vmap(one_row)(row_keys)
    return rows.reshape(N_GY * CY, N_GX).astype(jnp.int32)


def draw_fold_partner_column(key, part):
    offset = jax.random.randint(jax.random.fold_in(key, 5), (), 0, NX, dtype=jnp.int32)
    return ((offset - jnp.arange(NX, dtype=jnp.int32)) % NX).astype(jnp.int32)


def touch_ends(drawn, rng, least, top_value):
    spot = [jax.random.randint(jax.random.fold_in(rng, axis), (), 0, length) for axis, length in enumerate(drawn.shape)]
    widest = drawn.shape.index(max(drawn.shape))
    beside = spot[:widest] + [(spot[widest] + 1) % drawn.shape[widest]] + spot[widest + 1:]
    return drawn.at[tuple(spot)].set(least).at[tuple(beside)].set(top_value)


def block_scale(rng, extent, shards, least, largest):
    factor_of = 1.0
    for dim, shards_of in shards:
        steps = jax.random.uniform(jax.random.fold_in(jax.random.fold_in(rng, 6), dim), (shards_of,), jnp.float32, least / len(shards), largest / len(shards))
        factor_of = factor_of * jnp.repeat(jnp.exp(steps), extent[dim] // shards_of).reshape((-1,) + (1,) * (len(extent) - 1 - dim))
    return factor_of


def gaussian(own_key, dims, scale, limit, shards=(), kind=jnp.bfloat16):
    values = jax.random.normal(own_key, dims, jnp.float32) * scale
    if len(shards) > 0:
        values = block_scale(own_key, dims, shards, -0.22, 0.18) * values
    return jnp.clip(values, min=-limit, max=limit).astype(kind)


def setup_inputs(seed: int = 0) -> dict:
    arg_keys = jax.random.split(jax.random.key(seed), 12)
    ocean_blocks = gaussian(arg_keys[0], (NY, 4, NX), 1.0, 4.0, ((0, 4), (2, 8)), jnp.float32)
    block_map = draw_block_map(jax.random.fold_in(arg_keys[11], 71), 0)
    velocity = gaussian(arg_keys[2], (2, NY, NX), 0.3, 2.0, ((1, 4), (2, 8)), jnp.float32)
    stress = gaussian(arg_keys[3], (3, NY, NX), 0.5, 3.0, ((1, 4), (2, 8)), jnp.float32)
    thickness = jnp.clip(jnp.exp(math.log(5.0) - 4.6051702 * jax.random.uniform(arg_keys[4], (NCAT, NY, NX), jnp.float32) ** block_scale(arg_keys[4], (NCAT, NY, NX), ((1, 4), (2, 8)), -0.2, 0.2)), 0.05, 5.0)
    area = jnp.clip(0.1 + 0.1 * jax.random.uniform(arg_keys[5], (NCAT, NY, NX), jnp.float32) ** block_scale(arg_keys[5], (NCAT, NY, NX), ((1, 4), (2, 8)), -0.2, 0.2), 0.1, 0.2)
    wind = gaussian(arg_keys[6], (2, NY, NX), 0.5, 3.0, ((1, 4), (2, 8)), jnp.float32)
    air_temp = jnp.clip(-6.0 + 6.0 * jax.random.uniform(arg_keys[7], (NY, NX), jnp.float32) ** block_scale(arg_keys[7], (NY, NX), ((0, 4), (1, 8)), -0.2, 0.2), -6.0, 0.0)
    ice_presence_mask = touch_ends((jax.random.randint(arg_keys[8], (NY, NX), 0, 4) < 3).astype(jnp.int32), jax.random.fold_in(arg_keys[8], 1), 0, 1)
    ocean_land_mask = touch_ends((jax.random.randint(arg_keys[9], (NY, NX), 0, 10) < 9).astype(jnp.int32), jax.random.fold_in(arg_keys[9], 1), 0, 1)
    fold_partner_column = draw_fold_partner_column(jax.random.fold_in(arg_keys[11], 71), 0)
    return {"ocean_blocks": ocean_blocks, "block_map": block_map, "velocity": velocity, "stress": stress, "thickness": thickness, "area": area, "wind": wind, "air_temp": air_temp, "ice_presence_mask": ice_presence_mask, "ocean_land_mask": ocean_land_mask, "fold_partner_column": fold_partner_column}


RELAX = 0.5
ECC2 = 4.0
DMIN2 = 0.01
PSTAR = 1.0
CSTAR = 5.0
DTE = 0.3
DRAG = 1.0
FCOR = 0.5
KAPPA = 0.5
GAMMA = 0.3
DTT = 0.5
SREF = 34.0

def regroup(ocean_blocks, block_map):
    source = ocean_blocks.reshape(N_GY, CY, 4, N_GX, CX).transpose(0, 3, 1, 2, 4).reshape(N_GY, N_GX * CY, 4, CX)
    target = block_map.reshape(N_GY, CY, N_GX).transpose(0, 2, 1).reshape(N_GY, N_GX * CY)
    row_select = jnp.arange(N_GY, dtype=jnp.int32)[:, None]
    placed = jnp.zeros_like(source).at[row_select, target].set(source)
    return placed.reshape(N_GY, N_GX, CY, 4, CX).transpose(0, 2, 3, 1, 4).reshape(NY, 4, NX)

def global_rim_field(field, signs, fold_partner_column):
    columns = jnp.arange(-1, NX + 1, dtype=jnp.int32) % NX
    middle = jnp.take(field, columns, axis=2)
    north = jnp.take(field[:, NY - 1:NY, :], fold_partner_column[columns], axis=2) * signs
    south = jnp.zeros_like(north)
    return jnp.concatenate([south, middle, north], axis=1)

def compute_strain_rates(u_pad, v_pad):
    strain_rate_east = (u_pad[1:-1, 2:] - u_pad[1:-1, :-2]) * 0.5
    strain_rate_north = (v_pad[2:, 1:-1] - v_pad[:-2, 1:-1]) * 0.5
    strain_rate_shear = (u_pad[2:, 1:-1] - u_pad[:-2, 1:-1] + (v_pad[1:-1, 2:] - v_pad[1:-1, :-2])) * 0.25
    return (strain_rate_east, strain_rate_north, strain_rate_shear)

def stress_update(old, strain_rate_east, strain_rate_north, strain_rate_shear, strength):
    divergence = strain_rate_east + strain_rate_north
    tension = strain_rate_east - strain_rate_north
    shear = 2.0 * strain_rate_shear
    delta = jnp.sqrt(divergence * divergence + (tension * tension + shear * shear) / ECC2 + DMIN2)
    zeta = strength / delta
    first = (old[0] + RELAX * (zeta * divergence - strength)) / (1.0 + RELAX)
    second = (old[1] + RELAX * zeta * tension / ECC2) / (1.0 + RELAX)
    third = (old[2] + RELAX * zeta * shear / (2.0 * ECC2)) / (1.0 + RELAX)
    return jnp.stack([first, second, third])

def stress_force(padded):
    normal_x = (padded[0] + padded[1]) * 0.5
    normal_y = (padded[0] - padded[1]) * 0.5
    shear = padded[2]
    eastward_force = (normal_x[1:-1, 2:] - normal_x[1:-1, :-2]) * 0.5 + (shear[2:, 1:-1] - shear[:-2, 1:-1]) * 0.5
    northward_force = (shear[1:-1, 2:] - shear[1:-1, :-2]) * 0.5 + (normal_y[2:, 1:-1] - normal_y[:-2, 1:-1]) * 0.5
    return (eastward_force, northward_force)

def momentum_solve(velocity, eastward_force, northward_force, wind, ocean_current_east, ocean_current_north, ice_mass_per_area, coriolis_parameter, velocity_mask):
    east = velocity[0]
    north = velocity[1]
    implicit_denominator = ice_mass_per_area + DTE * DRAG
    right_side_east = east * ice_mass_per_area + DTE * (eastward_force + wind[0] + DRAG * ocean_current_east + ice_mass_per_area * coriolis_parameter * north)
    right_side_north = north * ice_mass_per_area + DTE * (northward_force + wind[1] + DRAG * ocean_current_north - ice_mass_per_area * coriolis_parameter * east)
    return jnp.stack([velocity_mask * right_side_east / implicit_denominator, velocity_mask * right_side_north / implicit_denominator])

def column_growth(thickness, velocity, ocean_temp, ocean_salt, ocean_current_east, ocean_current_north, air_temp, omask):
    freeze = -0.054 * (SREF + ocean_salt)
    rel_east = velocity[0] - ocean_current_east
    rel_north = velocity[1] - ocean_current_north
    speed = jnp.sqrt(rel_east * rel_east + rel_north * rel_north + 0.01)
    melt = GAMMA * (ocean_temp - freeze) * speed
    growth = KAPPA * (freeze - air_temp) / (thickness + 0.1)
    return omask * jnp.maximum(thickness + DTT * (growth - melt), 0.0)

def reference(ocean_blocks, block_map, velocity, stress, thickness, area, wind, air_temp, ice_presence_mask, ocean_land_mask, fold_partner_column):
    ocean = regroup(ocean_blocks, block_map)
    ocean_temp = ocean[:, 0, :]
    ocean_salt = ocean[:, 1, :]
    ocean_current_east = ocean[:, 2, :]
    ocean_current_north = ocean[:, 3, :]
    hsum = lax.optimization_barrier(jnp.sum(area * thickness, axis=0))
    conc = lax.optimization_barrier(jnp.sum(area, axis=0))
    strength = PSTAR * hsum * jnp.exp(-CSTAR * (1.0 - conc))
    ice_mass_per_area = hsum + 0.2
    row_float = jnp.arange(NY, dtype=jnp.int32).astype(jnp.float32)
    coriolis_parameter = (FCOR * (row_float + 0.5) / float(NY))[:, None]
    velocity_mask = (ice_presence_mask * ocean_land_mask).astype(jnp.float32)
    omask = ocean_land_mask.astype(jnp.float32)
    velocity_fold_sign = jnp.array([-1.0, -1.0], dtype=jnp.float32).reshape(2, 1, 1)
    ssign = jnp.ones((3, 1, 1), dtype=jnp.float32)
    for step in range(ITERS):
        velocity_padded = global_rim_field(velocity, velocity_fold_sign, fold_partner_column)
        strain_rate_east, strain_rate_north, strain_rate_shear = compute_strain_rates(velocity_padded[0], velocity_padded[1])
        stress = stress_update(stress, strain_rate_east, strain_rate_north, strain_rate_shear, strength)
        spad = global_rim_field(stress, ssign, fold_partner_column)
        eastward_force, northward_force = stress_force(spad)
        velocity = momentum_solve(velocity, eastward_force, northward_force, wind, ocean_current_east, ocean_current_north, ice_mass_per_area, coriolis_parameter, velocity_mask)
    thickness_out = column_growth(thickness, velocity, ocean_temp, ocean_salt, ocean_current_east, ocean_current_north, air_temp, omask)
    return (velocity, stress, thickness_out)
```

```python
import functools

import jax
import jax.numpy as jnp
from jax import lax
from jax.experimental import pallas as pl
from jax.experimental.pallas import tpu as pltpu
from jax.sharding import PartitionSpec as P

ITERS = 4
HALO = 8
MESH = pl.DeviceIdType.MESH
F32 = jnp.float32
DIRS = ((0, 1), (0, -1), (1, 0), (1, 1), (1, -1), (-1, 0), (-1, 1), (-1, -1))


def exact_dot(a, b, contract):
    return lax.dot_general(
        a,
        b,
        ((contract, (0,)), ((), ())),
        precision=lax.Precision.HIGHEST,
        preferred_element_type=F32,
    )


def each(count, fn):
    if count <= 8:
        for i in range(1, count):
            fn(i)
    else:
        lax.fori_loop(1, count, lambda i, c: (fn(i), c)[1], 0)


def flip8(x):
    row = lax.broadcasted_iota(jnp.int32, x.shape, 0)
    x = pltpu.roll(x, 4, axis=0)
    x = jnp.where((row // 2) % 2 == 0, pltpu.roll(x, 6, axis=0), pltpu.roll(x, 2, axis=0))
    return jnp.where(row % 2 == 0, pltpu.roll(x, 7, axis=0), pltpu.roll(x, 1, axis=0))


def pack(tiles):
    lane = lax.broadcasted_iota(jnp.int32, tiles[0].shape, 1) // 16
    out = pltpu.roll(tiles[0], 8, axis=1)
    for t in range(1, len(tiles)):
        out = jnp.where(lane == t, pltpu.roll(tiles[t], (8 + 16 * t) % 128, axis=1), out)
    return out


def unpack(west, east, count):
    lane = lax.broadcasted_iota(jnp.int32, west.shape, 1) % 16
    both = jnp.where(lane < 8, west, east)
    return [pltpu.roll(both, (120 - 16 * t) % 128, axis=1) for t in range(count)]


def kernel(
    n,
    m,
    ocean_ref,
    map_ref,
    vel_ref,
    str_ref,
    thick_ref,
    area_ref,
    wind_ref,
    air_ref,
    ice_ref,
    land_ref,
    fold_ref,
    vel_out,
    str_out,
    thick_out,
    ext,
    lext,
    a2a_out,
    a2a_in,
    ex_out,
    ex_in,
    ey_out,
    ey_in,
    ec_out,
    ec_in,
    lx_out,
    lx_in,
    ly_out,
    ly_in,
    lc_out,
    lc_in,
    efold_out,
    efold,
    lfold_out,
    lfold,
    a2a_ss,
    a2a_rs,
    e_ss,
    e_rs,
    l_ss,
    l_rs,
    ef_ss,
    ef_rs,
    lf_ss,
    lf_rs,
):
    rows, cols = air_ref.shape
    group = a2a_out.shape[2]
    gy = lax.axis_index("gy")
    gx = lax.axis_index("gx")
    last = m - 1
    top = gy == last
    has_n = gy < last
    has_s = gy > 0
    barrier = pltpu.get_barrier_semaphore()

    def gxi(off):
        return lax.rem(gx + off + n, n)

    def greet(off):
        pl.semaphore_signal(barrier, inc=1, device_id=(gy, gxi(off)), device_id_type=MESH)

    each(n, greet)
    for dy, cond in ((1, has_n), (-1, has_s)):

        @pl.when(cond)
        def _():
            for dx in (-1, 0, 1):
                pl.semaphore_signal(
                    barrier, inc=1, device_id=(gy + dy, gxi(dx)), device_id_type=MESH
                )

    target = map_ref[...]
    pos = (target // rows) * group + lax.rem(target, group)
    lanes = -(-(n * group) // 128) * 128
    sel_t = (pos == lax.broadcasted_iota(jnp.int32, (rows, lanes), 1)).astype(F32)
    slot_group = lax.broadcasted_iota(jnp.int32, (rows, cols), 0) // group + 1
    fields = [ocean_ref[:, f, :] for f in range(4)] + [slot_group.astype(F32)]
    for f in range(5):
        sorted_f = exact_dot(sel_t, fields[f], (0,))
        for p in range(n):
            a2a_out[p, f] = sorted_f[p * group : (p + 1) * group, :]

    count = (n - 1) + jnp.where(has_n, 3, 0) + jnp.where(has_s, 3, 0)
    pl.semaphore_wait(barrier, count)

    def a2a(off):
        return pltpu.make_async_remote_copy(
            src_ref=a2a_out.at[gxi(off)],
            dst_ref=a2a_in.at[off],
            send_sem=a2a_ss.at[off],
            recv_sem=a2a_rs.at[off],
            device_id=(gy, gxi(off)),
            device_id_type=MESH,
        )

    each(n, lambda off: a2a(off).start())

    area = [area_ref[c] for c in range(area_ref.shape[0])]
    thick = [thick_ref[c] for c in range(area_ref.shape[0])]
    hsum = area[0] * thick[0]
    conc = area[0]
    for c in range(1, len(area)):
        hsum = hsum + area[c] * thick[c]
        conc = conc + area[c]
    strength = hsum * jnp.exp(-5.0 * (1.0 - conc))
    mass = hsum + 0.2
    vmask = (ice_ref[...] * land_ref[...]).astype(F32)
    coef = vmask / (mass + 0.3)
    early = [
        vel_ref[0],
        vel_ref[1],
        str_ref[0],
        str_ref[1],
        str_ref[2],
        strength,
        coef * mass,
        coef * 0.3,
    ]
    esigns = (-1.0, -1.0, 1.0, 1.0, 1.0, 1.0, 1.0, 1.0)
    lsigns = (-1.0, -1.0)

    def prepare(vals, signs, e, x_out, y_out, c_out, fold_out, fold):
        tiles = rows // 8
        for f, val in enumerate(vals):
            e[f, HALO : HALO + rows, cols:] = val
            x_out[f] = pack([val[8 * t : 8 * t + 8] for t in range(tiles)])
            y_out[0, f] = val[rows - 8 :]
            y_out[1, f] = val[:8]
        c_out[0] = pack([val[rows - 8 :] for val in vals])
        c_out[1] = pack([val[:8] for val in vals])

        @pl.when(top)
        def _():
            for f in range(len(vals)):
                mirrored = flip8(y_out[0, f]) * signs[f]
                fold_out[f] = mirrored
                fold[0, f] = mirrored

    def halo(d, x_out, x_in, y_out, y_in, c_out, c_in, ss, rs):
        dy, dx = DIRS[d]
        if dy == 0:
            src, dst = x_out, x_in.at[0 if dx == 1 else 1]
        elif dx == 0:
            which = 0 if dy == 1 else 1
            src, dst = y_out.at[which], y_in.at[which]
        else:
            which = 0 if dy == 1 else 1
            src, dst = c_out.at[which], c_in.at[which, 0 if dx == 1 else 1]
        return pltpu.make_async_remote_copy(
            src_ref=src,
            dst_ref=dst,
            send_sem=ss.at[d],
            recv_sem=rs.at[d],
            device_id=(gy + dy, gxi(dx)),
            device_id_type=MESH,
        )

    def folding(off, fold_out, fold, ss, rs):
        return pltpu.make_async_remote_copy(
            src_ref=fold_out,
            dst_ref=fold.at[off],
            send_sem=ss.at[off],
            recv_sem=rs.at[off],
            device_id=(gy, gxi(off)),
            device_id_type=MESH,
        )

    def start(hargs, fargs):
        @pl.when(top)
        def _():
            each(n, lambda off: folding(off, *fargs).start())

        for d in (0, 1):
            halo(d, *hargs).start()

        @pl.when(has_n)
        def _():
            for d in (2, 3, 4):
                halo(d, *hargs).start()

        @pl.when(has_s)
        def _():
            for d in (5, 6, 7):
                halo(d, *hargs).start()

    def wait_sends(hargs, fargs):
        @pl.when(top)
        def _():
            each(n, lambda off: folding(off, *fargs).wait_send())

        for d in (0, 1):
            halo(d, *hargs).wait_send()

        @pl.when(has_n)
        def _():
            for d in (2, 3, 4):
                halo(d, *hargs).wait_send()

        @pl.when(has_s)
        def _():
            for d in (5, 6, 7):
                halo(d, *hargs).wait_send()

    def receive(nf, e, hargs, fargs):
        _, x_in, _, y_in, _, c_in, _, _ = hargs
        _, fold, _, _ = fargs
        for d in (0, 1):
            halo(d, *hargs).wait_recv()
        for f in range(nf):
            for t, tile in enumerate(unpack(x_in[0, f], x_in[1, f], rows // 8)):
                e[f, HALO + 8 * t : HALO + 8 * t + 8, :cols] = tile

        @pl.when(has_s)
        def _():
            for d in (2, 3, 4):
                halo(d, *hargs).wait_recv()
            corner = unpack(c_in[0, 0], c_in[0, 1], nf)
            for f in range(nf):
                e[f, :HALO, cols:] = y_in[0, f]
                e[f, :HALO, :cols] = corner[f]

        @pl.when(gy == 0)
        def _():
            for f in range(nf):
                e[f, :HALO, :] = jnp.zeros((HALO, 2 * cols), F32)

        @pl.when(has_n)
        def _():
            for d in (5, 6, 7):
                halo(d, *hargs).wait_recv()
            corner = unpack(c_in[1, 0], c_in[1, 1], nf)
            for f in range(nf):
                e[f, HALO + rows :, cols:] = y_in[1, f]
                e[f, HALO + rows :, :cols] = corner[f]

        @pl.when(top)
        def _():
            each(n, lambda off: folding(off, *fargs).wait_recv())
            total = n * cols
            c = fold_ref[0]
            base = c - (gx + 1) * cols - 8 + 2 * total
            first = base // cols
            lane = lax.broadcasted_iota(jnp.int32, (3 * cols, 2 * cols), 1)
            kk = lax.broadcasted_iota(jnp.int32, (3 * cols, 2 * cols), 0)
            column = gx * cols + lane - cols + jnp.where(lane < cols // 2, 2 * cols, 0)
            rel = c + 2 * total - column - first * cols
            picks = (kk == rel).astype(F32)
            blocks = []
            for b in range(3):
                slot = lax.rem(gx + 4 * n - first - b, n)
                blocks.append(fold[slot].reshape(nf * 8, cols))
            north = exact_dot(jnp.concatenate(blocks, axis=1), picks, (1,))
            for f in range(nf):
                e[f, HALO + rows :, :] = north[8 * f : 8 * f + 8, :]

    eargs = (ex_out, ex_in, ey_out, ey_in, ec_out, ec_in, e_ss, e_rs)
    efargs = (efold_out, efold, ef_ss, ef_rs)
    largs = (lx_out, lx_in, ly_out, ly_in, lc_out, lc_in, l_ss, l_rs)
    lfargs = (lfold_out, lfold, lf_ss, lf_rs)
    prepare(early, esigns, ext, ex_out, ey_out, ec_out, efold_out, efold)
    start(eargs, efargs)

    a2a_in[0] = a2a_out[gx]
    row_group = lax.broadcasted_iota(jnp.int32, (rows, cols), 0) // group + 1
    row_group = row_group.astype(F32)

    def place(i, acc):
        label = jnp.concatenate([a2a_in[i, 4]] * (rows // group), axis=0)
        hit = label == row_group
        return tuple(
            jnp.where(hit, jnp.concatenate([a2a_in[i, f]] * (rows // group), axis=0), acc[f])
            for f in range(4)
        )

    acc = tuple(jnp.zeros((rows, cols), F32) for _ in range(4))
    each(n, lambda off: a2a(off).wait_recv())
    if n <= 8:
        for i in range(n):
            acc = place(i, acc)
    else:
        acc = lax.fori_loop(0, n, place, acc)
    temp, salt, east, north = acc
    late = [wind_ref[0] + east, wind_ref[1] + north]
    prepare(late, lsigns, lext, lx_out, ly_out, lc_out, lfold_out, lfold)
    start(largs, lfargs)

    freeze = -0.054 * (34.0 + salt)
    excess = 0.15 * (temp - freeze)
    gap = 0.25 * (freeze - air_ref[...])
    for c in range(thick_ref.shape[0]):
        h = thick_ref[c]
        thick_out[c] = h + gap / (h + 0.1)

    receive(8, ext, eargs, efargs)
    u, v, s1, s2, s3, strn, ca, cb = [ext[f] for f in range(8)]
    wide = (rows + 2 * HALO, 2 * cols)
    g1 = g2 = cc = None
    for step in range(ITERS):
        ue = pltpu.roll(u, wide[1] - 1, axis=1) - pltpu.roll(u, 1, axis=1)
        vn = pltpu.roll(v, wide[0] - 1, axis=0) - pltpu.roll(v, 1, axis=0)
        un = pltpu.roll(u, wide[0] - 1, axis=0) - pltpu.roll(u, 1, axis=0)
        ve = pltpu.roll(v, wide[1] - 1, axis=1) - pltpu.roll(v, 1, axis=1)
        div = (ue + vn) * 0.5
        ten = (ue - vn) * 0.5
        she = (un + ve) * 0.5
        zeta = strn * lax.rsqrt(div * div + (ten * ten + she * she) * 0.25 + 0.01)
        s1 = s1 * (2.0 / 3.0) + (zeta * div - strn) * (1.0 / 3.0)
        s2 = s2 * (2.0 / 3.0) + zeta * ten * (1.0 / 12.0)
        s3 = s3 * (2.0 / 3.0) + zeta * she * (1.0 / 24.0)
        if step == 0:
            receive(2, lext, largs, lfargs)
            g1, g2 = lext[0], lext[1]
            grow = gy * rows - HALO + lax.broadcasted_iota(jnp.int32, wide, 0)
            grow = jnp.where(grow >= m * rows, 2 * m * rows - 1 - grow, grow)
            cc = ca * ((0.3 * 0.5 / (m * rows)) * (grow.astype(F32) + 0.5))
        sx = s1 + s2
        sy = s1 - s2
        fx = (pltpu.roll(sx, wide[1] - 1, axis=1) - pltpu.roll(sx, 1, axis=1)) * 0.25 + (
            pltpu.roll(s3, wide[0] - 1, axis=0) - pltpu.roll(s3, 1, axis=0)
        ) * 0.5
        fy = (pltpu.roll(s3, wide[1] - 1, axis=1) - pltpu.roll(s3, 1, axis=1)) * 0.5 + (
            pltpu.roll(sy, wide[0] - 1, axis=0) - pltpu.roll(sy, 1, axis=0)
        ) * 0.25
        u, v = ca * u + cc * v + cb * (fx + g1), ca * v - cc * u + cb * (fy + g2)

    inner = slice(HALO, HALO + rows)
    vel_out[0] = u[inner, cols:]
    vel_out[1] = v[inner, cols:]
    str_out[0] = s1[inner, cols:]
    str_out[1] = s2[inner, cols:]
    str_out[2] = s3[inner, cols:]
    de = u[inner, cols:] - east
    dn = v[inner, cols:] - north
    melt = excess * jnp.sqrt(de * de + dn * dn + 0.01)
    land = land_ref[...].astype(F32)
    for c in range(thick_ref.shape[0]):
        thick_out[c] = land * jnp.maximum(thick_out[c] - melt, 0.0)

    each(n, lambda off: a2a(off).wait_send())
    wait_sends(eargs, efargs)
    wait_sends(largs, lfargs)


def body(n, m, *args):
    ocean, block_map, vel, stress, thick = args[:5]
    rows, cols = args[7].shape
    group = max(2, rows // n)
    nf, nl = 8, 2
    wide = (rows + 2 * HALO, 2 * cols)
    vmem = pl.BlockSpec(memory_space=pltpu.VMEM)
    smem = pl.BlockSpec(memory_space=pltpu.SMEM)

    def bufs(k):
        return [
            pltpu.VMEM((k, 8, cols), F32),
            pltpu.VMEM((2, k, 8, cols), F32),
            pltpu.VMEM((2, k, 8, cols), F32),
            pltpu.VMEM((2, k, 8, cols), F32),
            pltpu.VMEM((2, 8, cols), F32),
            pltpu.VMEM((2, 2, 8, cols), F32),
        ]

    dma = pltpu.SemaphoreType.DMA
    return pl.pallas_call(
        functools.partial(kernel, n, m),
        out_shape=(
            jax.ShapeDtypeStruct(vel.shape, F32),
            jax.ShapeDtypeStruct(stress.shape, F32),
            jax.ShapeDtypeStruct(thick.shape, F32),
        ),
        in_specs=[vmem] * 10 + [smem],
        out_specs=(vmem, vmem, vmem),
        scratch_shapes=[
            pltpu.VMEM((nf,) + wide, F32),
            pltpu.VMEM((nl,) + wide, F32),
            pltpu.VMEM((n, 5, group, cols), F32),
            pltpu.VMEM((n, 5, group, cols), F32),
            *bufs(nf),
            *bufs(nl),
            pltpu.VMEM((nf, 8, cols), F32),
            pltpu.VMEM((n, nf, 8, cols), F32),
            pltpu.VMEM((nl, 8, cols), F32),
            pltpu.VMEM((n, nl, 8, cols), F32),
            dma((n,)),
            dma((n,)),
            dma((8,)),
            dma((8,)),
            dma((8,)),
            dma((8,)),
            dma((n,)),
            dma((n,)),
            dma((n,)),
            dma((n,)),
        ],
        compiler_params=pltpu.CompilerParams(
            collective_id=0, has_side_effects=True, vmem_limit_bytes=24 * 1024 * 1024
        ),
    )(*args)


def solution(mesh):
    placed = (
        P("gy", None, "gx"),
        P("gy", "gx"),
        P(None, "gy", "gx"),
        P(None, "gy", "gx"),
        P(None, "gy", "gx"),
        P(None, "gy", "gx"),
        P(None, "gy", "gx"),
        P("gy", "gx"),
        P("gy", "gx"),
        P("gy", "gx"),
        P(),
    )
    return jax.shard_map(
        functools.partial(body, mesh.shape["gx"], mesh.shape["gy"]),
        mesh=mesh,
        in_specs=placed,
        out_specs=(P(None, "gy", "gx"), P(None, "gy", "gx"), P(None, "gy", "gx")),
        check_vma=False,
    )
```

```python
import functools

import jax
import jax.numpy as jnp
from jax import lax
from jax.experimental import pallas as pl
from jax.experimental.pallas import tpu as pltpu
from jax.sharding import PartitionSpec as P

ITERS = 4
HALO = 8
MESH = pl.DeviceIdType.MESH
F32 = jnp.float32
DIRS = ((0, 1), (0, -1), (1, 0), (1, 1), (1, -1), (-1, 0), (-1, 1), (-1, -1))


def pieces(x):
    high = x.astype(jnp.bfloat16)
    rest = x - high.astype(F32)
    middle = rest.astype(jnp.bfloat16)
    low = (rest - middle.astype(F32)).astype(jnp.bfloat16)
    return high, middle, low


def dot(a, b):
    return jnp.dot(a, b, preferred_element_type=F32)


def each(count, fn):
    if count <= 8:
        for i in range(1, count):
            fn(i)
    else:
        lax.fori_loop(1, count, lambda i, c: (fn(i), c)[1], 0)


def flip8(x):
    row = lax.broadcasted_iota(jnp.int32, x.shape, 0)
    x = pltpu.roll(x, 4, axis=0)
    x = jnp.where((row // 2) % 2 == 0, pltpu.roll(x, 6, axis=0), pltpu.roll(x, 2, axis=0))
    return jnp.where(row % 2 == 0, pltpu.roll(x, 7, axis=0), pltpu.roll(x, 1, axis=0))


def pack(tiles):
    lane = lax.broadcasted_iota(jnp.int32, tiles[0].shape, 1) // 16
    out = pltpu.roll(tiles[0], 8, axis=1)
    for t in range(1, len(tiles)):
        out = jnp.where(lane == t, pltpu.roll(tiles[t], (8 + 16 * t) % 128, axis=1), out)
    return out


def unpack(west, east, count):
    lane = lax.broadcasted_iota(jnp.int32, west.shape, 1) % 16
    both = jnp.where(lane < 8, west, east)
    return [pltpu.roll(both, (120 - 16 * t) % 128, axis=1) for t in range(count)]


def kernel(
    n,
    m,
    ocean_hbm,
    map_hbm,
    vel_hbm,
    str_hbm,
    thick_hbm,
    area_hbm,
    wind_hbm,
    air_hbm,
    ice_hbm,
    land_hbm,
    fold_hbm,
    vel_out,
    str_out,
    thick_out,
    ocean_ref,
    map_ref,
    vel_ref,
    str_ref,
    thick_ref,
    area_ref,
    wind_ref,
    air_ref,
    ice_ref,
    land_ref,
    fold_ref,
    in_sem,
    ext,
    lext,
    a2a_out,
    a2a_in,
    ex_out,
    ex_in,
    ey_out,
    ey_in,
    ec_out,
    ec_in,
    lx_out,
    lx_in,
    ly_out,
    ly_in,
    lc_out,
    lc_in,
    efold_out,
    efold,
    lfold_out,
    lfold,
    a2a_ss,
    a2a_rs,
    e_ss,
    e_rs,
    l_ss,
    l_rs,
    ef_ss,
    ef_rs,
    lf_ss,
    lf_rs,
):
    rows, cols = air_ref.shape
    group = a2a_out.shape[2]
    gy = lax.axis_index("gy")
    gx = lax.axis_index("gx")
    last = m - 1
    top = gy == last
    has_n = gy < last
    has_s = gy > 0
    barrier = pltpu.get_barrier_semaphore()

    def gxi(off):
        return lax.rem(gx + off + n, n)

    def greet(off):
        pl.semaphore_signal(barrier, inc=1, device_id=(gy, gxi(off)), device_id_type=MESH)

    each(n, greet)
    for dy, cond in ((1, has_n), (-1, has_s)):

        @pl.when(cond)
        def _():
            for dx in (-1, 0, 1):
                pl.semaphore_signal(
                    barrier, inc=1, device_id=(gy + dy, gxi(dx)), device_id_type=MESH
                )

    pairs = (
        (ocean_hbm, ocean_ref),
        (map_hbm, map_ref),
        (area_hbm, area_ref),
        (thick_hbm, thick_ref),
        (vel_hbm, vel_ref),
        (str_hbm, str_ref),
        (ice_hbm, ice_ref),
        (land_hbm, land_ref),
        (wind_hbm, wind_ref),
        (air_hbm, air_ref),
        (fold_hbm, fold_ref),
    )
    loads = [pltpu.make_async_copy(src, dst, in_sem.at[i]) for i, (src, dst) in enumerate(pairs)]
    for load in loads:
        load.start()
    loads[0].wait()
    loads[1].wait()

    target = map_ref[...]
    pos = (target // rows) * group + lax.rem(target, group)
    order = lax.broadcasted_iota(jnp.int32, (n * group, rows), 0)
    picked = (jnp.broadcast_to(pos, (n * group, rows)) == order).astype(jnp.bfloat16)
    slot_group = lax.broadcasted_iota(jnp.int32, (rows, cols), 0) // group + 1
    fields = [ocean_ref[:, f, :] for f in range(4)] + [slot_group.astype(F32)]
    for f in range(5):
        if f < 4:
            high, middle, low = pieces(fields[f])
            sorted_f = (dot(picked, high) + dot(picked, middle)) + dot(picked, low)
        else:
            sorted_f = dot(picked, fields[f].astype(jnp.bfloat16))
        for p in range(n):
            a2a_out[p, f] = sorted_f[p * group : (p + 1) * group, :]

    count = (n - 1) + jnp.where(has_n, 3, 0) + jnp.where(has_s, 3, 0)
    pl.semaphore_wait(barrier, count)

    def a2a(off):
        return pltpu.make_async_remote_copy(
            src_ref=a2a_out.at[gxi(off)],
            dst_ref=a2a_in.at[off],
            send_sem=a2a_ss.at[off],
            recv_sem=a2a_rs.at[off],
            device_id=(gy, gxi(off)),
            device_id_type=MESH,
        )

    each(n, lambda off: a2a(off).start())
    for load in loads[2:]:
        load.wait()

    area = [area_ref[c] for c in range(area_ref.shape[0])]
    thick = [thick_ref[c] for c in range(area_ref.shape[0])]
    hsum = area[0] * thick[0]
    conc = area[0]
    for c in range(1, len(area)):
        hsum = hsum + area[c] * thick[c]
        conc = conc + area[c]
    strength = hsum * jnp.exp(-5.0 * (1.0 - conc))
    mass = hsum + 0.2
    vmask = (ice_ref[...] * land_ref[...]).astype(F32)
    coef = vmask / (mass + 0.3)
    early = [
        vel_ref[0],
        vel_ref[1],
        str_ref[0],
        str_ref[1],
        str_ref[2],
        strength,
        coef * mass,
        coef * 0.3,
    ]
    esigns = (-1.0, -1.0, 1.0, 1.0, 1.0, 1.0, 1.0, 1.0)
    lsigns = (-1.0, -1.0)

    def prepare(vals, signs, e, x_out, y_out, c_out, fold_out, fold):
        tiles = rows // 8
        for f, val in enumerate(vals):
            e[f, HALO : HALO + rows, cols:] = val
            x_out[f] = pack([val[8 * t : 8 * t + 8] for t in range(tiles)])
            y_out[0, f] = val[rows - 8 :]
            y_out[1, f] = val[:8]
        c_out[0] = pack([val[rows - 8 :] for val in vals])
        c_out[1] = pack([val[:8] for val in vals])

        @pl.when(top)
        def _():
            for f in range(len(vals)):
                mirrored = flip8(y_out[0, f]) * signs[f]
                fold_out[f] = mirrored
                fold[0, f] = mirrored

    def halo(d, x_out, x_in, y_out, y_in, c_out, c_in, ss, rs):
        dy, dx = DIRS[d]
        if dy == 0:
            src, dst = x_out, x_in.at[0 if dx == 1 else 1]
        elif dx == 0:
            which = 0 if dy == 1 else 1
            src, dst = y_out.at[which], y_in.at[which]
        else:
            which = 0 if dy == 1 else 1
            src, dst = c_out.at[which], c_in.at[which, 0 if dx == 1 else 1]
        return pltpu.make_async_remote_copy(
            src_ref=src,
            dst_ref=dst,
            send_sem=ss.at[d],
            recv_sem=rs.at[d],
            device_id=(gy + dy, gxi(dx)),
            device_id_type=MESH,
        )

    def folding(off, fold_out, fold, ss, rs):
        return pltpu.make_async_remote_copy(
            src_ref=fold_out,
            dst_ref=fold.at[off],
            send_sem=ss.at[off],
            recv_sem=rs.at[off],
            device_id=(gy, gxi(off)),
            device_id_type=MESH,
        )

    def start(hargs, fargs):
        @pl.when(top)
        def _():
            each(n, lambda off: folding(off, *fargs).start())

        for d in (0, 1):
            halo(d, *hargs).start()

        @pl.when(has_n)
        def _():
            for d in (2, 3, 4):
                halo(d, *hargs).start()

        @pl.when(has_s)
        def _():
            for d in (5, 6, 7):
                halo(d, *hargs).start()

    def wait_sends(hargs, fargs):
        @pl.when(top)
        def _():
            each(n, lambda off: folding(off, *fargs).wait_send())

        for d in (0, 1):
            halo(d, *hargs).wait_send()

        @pl.when(has_n)
        def _():
            for d in (2, 3, 4):
                halo(d, *hargs).wait_send()

        @pl.when(has_s)
        def _():
            for d in (5, 6, 7):
                halo(d, *hargs).wait_send()

    def receive(nf, e, hargs, fargs):
        _, x_in, _, y_in, _, c_in, _, _ = hargs
        _, fold, _, _ = fargs
        for d in (0, 1):
            halo(d, *hargs).wait_recv()
        for f in range(nf):
            for t, tile in enumerate(unpack(x_in[0, f], x_in[1, f], rows // 8)):
                e[f, HALO + 8 * t : HALO + 8 * t + 8, :cols] = tile

        @pl.when(has_s)
        def _():
            for d in (2, 3, 4):
                halo(d, *hargs).wait_recv()
            corner = unpack(c_in[0, 0], c_in[0, 1], nf)
            for f in range(nf):
                e[f, :HALO, cols:] = y_in[0, f]
                e[f, :HALO, :cols] = corner[f]

        @pl.when(gy == 0)
        def _():
            for f in range(nf):
                e[f, :HALO, :] = jnp.zeros((HALO, 2 * cols), F32)

        @pl.when(has_n)
        def _():
            for d in (5, 6, 7):
                halo(d, *hargs).wait_recv()
            corner = unpack(c_in[1, 0], c_in[1, 1], nf)
            for f in range(nf):
                e[f, HALO + rows :, cols:] = y_in[1, f]
                e[f, HALO + rows :, :cols] = corner[f]

        @pl.when(top)
        def _():
            each(n, lambda off: folding(off, *fargs).wait_recv())
            total = n * cols
            c = fold_ref[0]
            base = c - (gx + 1) * cols - 8 + 2 * total
            first = base // cols
            lane = lax.broadcasted_iota(jnp.int32, (3 * cols, 2 * cols), 1)
            kk = lax.broadcasted_iota(jnp.int32, (3 * cols, 2 * cols), 0)
            column = gx * cols + lane - cols + jnp.where(lane < cols // 2, 2 * cols, 0)
            rel = c + 2 * total - column - first * cols
            picks = (kk == rel).astype(jnp.bfloat16)
            blocks = []
            for b in range(3):
                slot = lax.rem(gx + 4 * n - first - b, n)
                blocks.append(fold[slot].reshape(nf * 8, cols))
            high, middle, low = pieces(jnp.concatenate(blocks, axis=1))
            north = (dot(high, picks) + dot(middle, picks)) + dot(low, picks)
            for f in range(nf):
                e[f, HALO + rows :, :] = north[8 * f : 8 * f + 8, :]

    eargs = (ex_out, ex_in, ey_out, ey_in, ec_out, ec_in, e_ss, e_rs)
    efargs = (efold_out, efold, ef_ss, ef_rs)
    largs = (lx_out, lx_in, ly_out, ly_in, lc_out, lc_in, l_ss, l_rs)
    lfargs = (lfold_out, lfold, lf_ss, lf_rs)
    prepare(early, esigns, ext, ex_out, ey_out, ec_out, efold_out, efold)
    start(eargs, efargs)

    a2a_in[0] = a2a_out[gx]
    row_group = lax.broadcasted_iota(jnp.int32, (rows, cols), 0) // group + 1
    row_group = row_group.astype(F32)

    def place(i, acc):
        label = jnp.concatenate([a2a_in[i, 4]] * (rows // group), axis=0)
        hit = label == row_group
        return tuple(
            jnp.where(hit, jnp.concatenate([a2a_in[i, f]] * (rows // group), axis=0), acc[f])
            for f in range(4)
        )

    acc = tuple(jnp.zeros((rows, cols), F32) for _ in range(4))
    each(n, lambda off: a2a(off).wait_recv())
    if n <= 8:
        for i in range(n):
            acc = place(i, acc)
    else:
        acc = lax.fori_loop(0, n, place, acc)
    temp, salt, east, north = acc
    late = [wind_ref[0] + east, wind_ref[1] + north]
    prepare(late, lsigns, lext, lx_out, ly_out, lc_out, lfold_out, lfold)
    start(largs, lfargs)

    freeze = -0.054 * (34.0 + salt)
    excess = 0.15 * (temp - freeze)
    gap = 0.25 * (freeze - air_ref[...])
    for c in range(thick_ref.shape[0]):
        h = thick_ref[c]
        thick_out[c] = h + gap / (h + 0.1)

    receive(8, ext, eargs, efargs)
    u, v, s1, s2, s3, strn, ca, cb = [ext[f] for f in range(8)]
    wide = (rows + 2 * HALO, 2 * cols)
    g1 = g2 = cc = None
    for step in range(ITERS):
        ue = pltpu.roll(u, wide[1] - 1, axis=1) - pltpu.roll(u, 1, axis=1)
        vn = pltpu.roll(v, wide[0] - 1, axis=0) - pltpu.roll(v, 1, axis=0)
        un = pltpu.roll(u, wide[0] - 1, axis=0) - pltpu.roll(u, 1, axis=0)
        ve = pltpu.roll(v, wide[1] - 1, axis=1) - pltpu.roll(v, 1, axis=1)
        div = (ue + vn) * 0.5
        ten = (ue - vn) * 0.5
        she = (un + ve) * 0.5
        zeta = strn * lax.rsqrt(div * div + (ten * ten + she * she) * 0.25 + 0.01)
        s1 = s1 * (2.0 / 3.0) + (zeta * div - strn) * (1.0 / 3.0)
        s2 = s2 * (2.0 / 3.0) + zeta * ten * (1.0 / 12.0)
        s3 = s3 * (2.0 / 3.0) + zeta * she * (1.0 / 24.0)
        if step == 0:
            receive(2, lext, largs, lfargs)
            g1, g2 = lext[0], lext[1]
            grow = gy * rows - HALO + lax.broadcasted_iota(jnp.int32, wide, 0)
            grow = jnp.where(grow >= m * rows, 2 * m * rows - 1 - grow, grow)
            cc = ca * ((0.3 * 0.5 / (m * rows)) * (grow.astype(F32) + 0.5))
        sx = s1 + s2
        sy = s1 - s2
        fx = (pltpu.roll(sx, wide[1] - 1, axis=1) - pltpu.roll(sx, 1, axis=1)) * 0.25 + (
            pltpu.roll(s3, wide[0] - 1, axis=0) - pltpu.roll(s3, 1, axis=0)
        ) * 0.5
        fy = (pltpu.roll(s3, wide[1] - 1, axis=1) - pltpu.roll(s3, 1, axis=1)) * 0.5 + (
            pltpu.roll(sy, wide[0] - 1, axis=0) - pltpu.roll(sy, 1, axis=0)
        ) * 0.25
        u, v = ca * u + cc * v + cb * (fx + g1), ca * v - cc * u + cb * (fy + g2)

    inner = slice(HALO, HALO + rows)
    vel_out[0] = u[inner, cols:]
    vel_out[1] = v[inner, cols:]
    str_out[0] = s1[inner, cols:]
    str_out[1] = s2[inner, cols:]
    str_out[2] = s3[inner, cols:]
    de = u[inner, cols:] - east
    dn = v[inner, cols:] - north
    melt = excess * jnp.sqrt(de * de + dn * dn + 0.01)
    land = land_ref[...].astype(F32)
    for c in range(thick_ref.shape[0]):
        thick_out[c] = land * jnp.maximum(thick_out[c] - melt, 0.0)

    each(n, lambda off: a2a(off).wait_send())
    wait_sends(eargs, efargs)
    wait_sends(largs, lfargs)


def body(n, m, *args):
    ocean, block_map, vel, stress, thick = args[:5]
    rows, cols = args[7].shape
    group = max(2, rows // n)
    nf, nl = 8, 2
    wide = (rows + 2 * HALO, 2 * cols)
    vmem = pl.BlockSpec(memory_space=pltpu.VMEM)
    hbm = pl.BlockSpec(memory_space=pltpu.MemorySpace.HBM)
    args = tuple(pltpu.with_memory_space_constraint(a, pltpu.MemorySpace.HBM) for a in (ocean, block_map.T) + args[2:])

    def bufs(k):
        return [
            pltpu.VMEM((k, 8, cols), F32),
            pltpu.VMEM((2, k, 8, cols), F32),
            pltpu.VMEM((2, k, 8, cols), F32),
            pltpu.VMEM((2, k, 8, cols), F32),
            pltpu.VMEM((2, 8, cols), F32),
            pltpu.VMEM((2, 2, 8, cols), F32),
        ]

    dma = pltpu.SemaphoreType.DMA
    return pl.pallas_call(
        functools.partial(kernel, n, m),
        out_shape=(
            jax.ShapeDtypeStruct(vel.shape, F32),
            jax.ShapeDtypeStruct(stress.shape, F32),
            jax.ShapeDtypeStruct(thick.shape, F32),
        ),
        in_specs=[hbm] * 11,
        out_specs=(vmem, vmem, vmem),
        scratch_shapes=[
            *[pltpu.VMEM(a.shape, a.dtype) for a in args[:10]],
            pltpu.SMEM(args[10].shape, jnp.int32),
            dma((11,)),
            pltpu.VMEM((nf,) + wide, F32),
            pltpu.VMEM((nl,) + wide, F32),
            pltpu.VMEM((n, 5, group, cols), F32),
            pltpu.VMEM((n, 5, group, cols), F32),
            *bufs(nf),
            *bufs(nl),
            pltpu.VMEM((nf, 8, cols), F32),
            pltpu.VMEM((n, nf, 8, cols), F32),
            pltpu.VMEM((nl, 8, cols), F32),
            pltpu.VMEM((n, nl, 8, cols), F32),
            dma((n,)),
            dma((n,)),
            dma((8,)),
            dma((8,)),
            dma((8,)),
            dma((8,)),
            dma((n,)),
            dma((n,)),
            dma((n,)),
            dma((n,)),
        ],
        compiler_params=pltpu.CompilerParams(
            collective_id=0, has_side_effects=True, vmem_limit_bytes=24 * 1024 * 1024
        ),
    )(*args)


def solution(mesh):
    placed = (
        P("gy", None, "gx"),
        P("gy", "gx"),
        P(None, "gy", "gx"),
        P(None, "gy", "gx"),
        P(None, "gy", "gx"),
        P(None, "gy", "gx"),
        P(None, "gy", "gx"),
        P("gy", "gx"),
        P("gy", "gx"),
        P("gy", "gx"),
        P(),
    )
    return jax.shard_map(
        functools.partial(body, mesh.shape["gx"], mesh.shape["gy"]),
        mesh=mesh,
        in_specs=placed,
        out_specs=(P(None, "gy", "gx"), P(None, "gy", "gx"), P(None, "gy", "gx")),
        check_vma=False,
    )
```

```python
import functools

import jax
import jax.numpy as jnp
from jax import lax
from jax.experimental import pallas as pl
from jax.experimental.pallas import tpu as pltpu
from jax.sharding import PartitionSpec as P

ITERS = 4
HALO = 8
MESH = pl.DeviceIdType.MESH
F32 = jnp.float32
DIRS = ((0, 1), (0, -1), (1, 0), (1, 1), (1, -1), (-1, 0), (-1, 1), (-1, -1))


def pieces(x):
    high = x.astype(jnp.bfloat16)
    rest = x - high.astype(F32)
    middle = rest.astype(jnp.bfloat16)
    low = (rest - middle.astype(F32)).astype(jnp.bfloat16)
    return high, middle, low


def dot(a, b):
    return jnp.dot(a, b, preferred_element_type=F32)


def each(count, fn):
    if count <= 8:
        for i in range(1, count):
            fn(i)
    else:
        lax.fori_loop(1, count, lambda i, c: (fn(i), c)[1], 0)


def flip8(x):
    row = lax.broadcasted_iota(jnp.int32, x.shape, 0)
    x = pltpu.roll(x, 4, axis=0)
    x = jnp.where((row // 2) % 2 == 0, pltpu.roll(x, 6, axis=0), pltpu.roll(x, 2, axis=0))
    return jnp.where(row % 2 == 0, pltpu.roll(x, 7, axis=0), pltpu.roll(x, 1, axis=0))


def pack(tiles):
    lane = lax.broadcasted_iota(jnp.int32, tiles[0].shape, 1) // 16
    out = pltpu.roll(tiles[0], 8, axis=1)
    for t in range(1, len(tiles)):
        out = jnp.where(lane == t, pltpu.roll(tiles[t], (8 + 16 * t) % 128, axis=1), out)
    return out


def unpack(west, east, count):
    lane = lax.broadcasted_iota(jnp.int32, west.shape, 1) % 16
    both = jnp.where(lane < 8, west, east)
    return [pltpu.roll(both, (120 - 16 * t) % 128, axis=1) for t in range(count)]


def kernel(
    n,
    m,
    ocean_hbm,
    map_hbm,
    vel_hbm,
    str_hbm,
    thick_hbm,
    area_hbm,
    wind_hbm,
    air_hbm,
    ice_hbm,
    land_hbm,
    fold_hbm,
    vel_out,
    str_out,
    thick_out,
    ocean_ref,
    map_ref,
    vel_ref,
    str_ref,
    thick_ref,
    area_ref,
    wind_ref,
    air_ref,
    ice_ref,
    land_ref,
    fold_ref,
    in_sem,
    picks_ref,
    ext,
    lext,
    a2a_out,
    a2a_in,
    ex_out,
    ex_in,
    ey_out,
    ey_in,
    ec_out,
    ec_in,
    lx_out,
    lx_in,
    ly_out,
    ly_in,
    lc_out,
    lc_in,
    efold_out,
    efold,
    lfold_out,
    lfold,
    a2a_ss,
    a2a_rs,
    e_ss,
    e_rs,
    l_ss,
    l_rs,
    ef_ss,
    ef_rs,
    lf_ss,
    lf_rs,
):
    rows, cols = air_ref.shape
    group = a2a_out.shape[2]
    gy = lax.axis_index("gy")
    gx = lax.axis_index("gx")
    last = m - 1
    top = gy == last
    has_n = gy < last
    has_s = gy > 0
    barrier = pltpu.get_barrier_semaphore()

    def gxi(off):
        return lax.rem(gx + off + n, n)

    def greet(off):
        pl.semaphore_signal(barrier, inc=1, device_id=(gy, gxi(off)), device_id_type=MESH)

    each(n, greet)
    for dy, cond in ((1, has_n), (-1, has_s)):

        @pl.when(cond)
        def _():
            for dx in (-1, 0, 1):
                pl.semaphore_signal(
                    barrier, inc=1, device_id=(gy + dy, gxi(dx)), device_id_type=MESH
                )

    pairs = (
        (ocean_hbm, ocean_ref),
        (map_hbm, map_ref),
        (area_hbm, area_ref),
        (thick_hbm, thick_ref),
        (vel_hbm, vel_ref),
        (str_hbm, str_ref),
        (ice_hbm, ice_ref),
        (land_hbm, land_ref),
        (wind_hbm, wind_ref),
        (air_hbm, air_ref),
        (fold_hbm, fold_ref),
    )
    loads = [pltpu.make_async_copy(src, dst, in_sem.at[i]) for i, (src, dst) in enumerate(pairs)]
    for load in loads:
        load.start()
    loads[0].wait()
    loads[1].wait()

    target = map_ref[...]
    pos = (target // rows) * group + lax.rem(target, group)
    order = lax.broadcasted_iota(jnp.int32, (n * group, rows), 0)
    picked = (jnp.broadcast_to(pos, (n * group, rows)) == order).astype(jnp.bfloat16)
    slot_group = lax.broadcasted_iota(jnp.int32, (rows, cols), 0) // group + 1
    fields = [ocean_ref[:, f, :] for f in range(4)] + [slot_group.astype(F32)]
    for f in range(5):
        if f < 4:
            high, middle, low = pieces(fields[f])
            sorted_f = (dot(picked, high) + dot(picked, middle)) + dot(picked, low)
        else:
            sorted_f = dot(picked, fields[f].astype(jnp.bfloat16))
        for p in range(n):
            a2a_out[p, f] = sorted_f[p * group : (p + 1) * group, :]

    count = (n - 1) + jnp.where(has_n, 3, 0) + jnp.where(has_s, 3, 0)
    pl.semaphore_wait(barrier, count)

    def a2a(off):
        return pltpu.make_async_remote_copy(
            src_ref=a2a_out.at[gxi(off)],
            dst_ref=a2a_in.at[off],
            send_sem=a2a_ss.at[off],
            recv_sem=a2a_rs.at[off],
            device_id=(gy, gxi(off)),
            device_id_type=MESH,
        )

    each(n, lambda off: a2a(off).start())
    for load in loads[2:]:
        load.wait()

    area = [area_ref[c] for c in range(area_ref.shape[0])]
    thick = [thick_ref[c] for c in range(area_ref.shape[0])]
    hsum = area[0] * thick[0]
    conc = area[0]
    for c in range(1, len(area)):
        hsum = hsum + area[c] * thick[c]
        conc = conc + area[c]
    strength = hsum * jnp.exp(-5.0 * (1.0 - conc))
    mass = hsum + 0.2
    vmask = (ice_ref[...] * land_ref[...]).astype(F32)
    coef = vmask / (mass + 0.3)
    early = [
        vel_ref[0],
        vel_ref[1],
        str_ref[0],
        str_ref[1],
        str_ref[2],
        strength,
        coef * mass,
        coef * 0.3,
    ]
    esigns = (-1.0, -1.0, 1.0, 1.0, 1.0, 1.0, 1.0, 1.0)
    lsigns = (-1.0, -1.0)

    def prepare(vals, signs, e, x_out, y_out, c_out, fold_out, fold):
        tiles = rows // 8
        for f, val in enumerate(vals):
            e[f, HALO : HALO + rows, cols:] = val
            x_out[f] = pack([val[8 * t : 8 * t + 8] for t in range(tiles)])
            y_out[0, f] = val[rows - 8 :]
            y_out[1, f] = val[:8]
        c_out[0] = pack([val[rows - 8 :] for val in vals])
        c_out[1] = pack([val[:8] for val in vals])

        @pl.when(top)
        def _():
            for f in range(len(vals)):
                mirrored = flip8(y_out[0, f]) * signs[f]
                fold_out[f] = mirrored
                fold[0, f] = mirrored

    def halo(d, x_out, x_in, y_out, y_in, c_out, c_in, ss, rs):
        dy, dx = DIRS[d]
        if dy == 0:
            src, dst = x_out, x_in.at[0 if dx == 1 else 1]
        elif dx == 0:
            which = 0 if dy == 1 else 1
            src, dst = y_out.at[which], y_in.at[which]
        else:
            which = 0 if dy == 1 else 1
            src, dst = c_out.at[which], c_in.at[which, 0 if dx == 1 else 1]
        return pltpu.make_async_remote_copy(
            src_ref=src,
            dst_ref=dst,
            send_sem=ss.at[d],
            recv_sem=rs.at[d],
            device_id=(gy + dy, gxi(dx)),
            device_id_type=MESH,
        )

    def folding(off, fold_out, fold, ss, rs):
        return pltpu.make_async_remote_copy(
            src_ref=fold_out,
            dst_ref=fold.at[off],
            send_sem=ss.at[off],
            recv_sem=rs.at[off],
            device_id=(gy, gxi(off)),
            device_id_type=MESH,
        )

    def start(hargs, fargs):
        @pl.when(top)
        def _():
            each(n, lambda off: folding(off, *fargs).start())

        for d in (0, 1):
            halo(d, *hargs).start()

        @pl.when(has_n)
        def _():
            for d in (2, 3, 4):
                halo(d, *hargs).start()

        @pl.when(has_s)
        def _():
            for d in (5, 6, 7):
                halo(d, *hargs).start()

    def wait_sends(hargs, fargs):
        @pl.when(top)
        def _():
            each(n, lambda off: folding(off, *fargs).wait_send())

        for d in (0, 1):
            halo(d, *hargs).wait_send()

        @pl.when(has_n)
        def _():
            for d in (2, 3, 4):
                halo(d, *hargs).wait_send()

        @pl.when(has_s)
        def _():
            for d in (5, 6, 7):
                halo(d, *hargs).wait_send()

    def first_block():
        return (fold_ref[0] - (gx + 1) * cols - 8 + 2 * n * cols) // cols

    def receive(nf, e, hargs, fargs):
        _, x_in, _, y_in, _, c_in, _, _ = hargs
        _, fold, _, _ = fargs
        for d in (0, 1):
            halo(d, *hargs).wait_recv()
        for f in range(nf):
            for t, tile in enumerate(unpack(x_in[0, f], x_in[1, f], rows // 8)):
                e[f, HALO + 8 * t : HALO + 8 * t + 8, :cols] = tile

        @pl.when(has_s)
        def _():
            for d in (2, 3, 4):
                halo(d, *hargs).wait_recv()
            corner = unpack(c_in[0, 0], c_in[0, 1], nf)
            for f in range(nf):
                e[f, :HALO, cols:] = y_in[0, f]
                e[f, :HALO, :cols] = corner[f]

        @pl.when(gy == 0)
        def _():
            for f in range(nf):
                e[f, :HALO, :] = jnp.zeros((HALO, 2 * cols), F32)

        @pl.when(has_n)
        def _():
            for d in (5, 6, 7):
                halo(d, *hargs).wait_recv()
            corner = unpack(c_in[1, 0], c_in[1, 1], nf)
            for f in range(nf):
                e[f, HALO + rows :, cols:] = y_in[1, f]
                e[f, HALO + rows :, :cols] = corner[f]

        @pl.when(top)
        def _():
            each(n, lambda off: folding(off, *fargs).wait_recv())
            first = first_block()
            picks = picks_ref[...]
            blocks = []
            for b in range(3):
                slot = lax.rem(gx + 4 * n - first - b, n)
                blocks.append(fold[slot].reshape(nf * 8, cols))
            high, middle, low = pieces(jnp.concatenate(blocks, axis=1))
            north = (dot(high, picks) + dot(middle, picks)) + dot(low, picks)
            for f in range(nf):
                e[f, HALO + rows :, :] = north[8 * f : 8 * f + 8, :]

    def build_picks():
        @pl.when(top)
        def _():
            first = first_block()
            lane = lax.broadcasted_iota(jnp.int32, (3 * cols, 2 * cols), 1)
            kk = lax.broadcasted_iota(jnp.int32, (3 * cols, 2 * cols), 0)
            column = gx * cols + lane - cols + jnp.where(lane < cols // 2, 2 * cols, 0)
            rel = fold_ref[0] + 2 * n * cols - column - first * cols
            picks_ref[...] = (kk == rel).astype(jnp.bfloat16)

    eargs = (ex_out, ex_in, ey_out, ey_in, ec_out, ec_in, e_ss, e_rs)
    efargs = (efold_out, efold, ef_ss, ef_rs)
    largs = (lx_out, lx_in, ly_out, ly_in, lc_out, lc_in, l_ss, l_rs)
    lfargs = (lfold_out, lfold, lf_ss, lf_rs)
    prepare(early, esigns, ext, ex_out, ey_out, ec_out, efold_out, efold)
    start(eargs, efargs)
    build_picks()

    a2a_in[0] = a2a_out[gx]
    row_group = lax.broadcasted_iota(jnp.int32, (rows, cols), 0) // group + 1
    row_group = row_group.astype(F32)

    def place(i, acc):
        label = jnp.concatenate([a2a_in[i, 4]] * (rows // group), axis=0)
        hit = label == row_group
        return tuple(
            jnp.where(hit, jnp.concatenate([a2a_in[i, f]] * (rows // group), axis=0), acc[f])
            for f in range(4)
        )

    acc = tuple(jnp.zeros((rows, cols), F32) for _ in range(4))
    each(n, lambda off: a2a(off).wait_recv())
    if n <= 8:
        for i in range(n):
            acc = place(i, acc)
    else:
        acc = lax.fori_loop(0, n, place, acc)
    temp, salt, east, north = acc
    late = [wind_ref[0] + east, wind_ref[1] + north]
    prepare(late, lsigns, lext, lx_out, ly_out, lc_out, lfold_out, lfold)
    start(largs, lfargs)

    freeze = -0.054 * (34.0 + salt)
    excess = 0.15 * (temp - freeze)
    gap = 0.25 * (freeze - air_ref[...])
    for c in range(thick_ref.shape[0]):
        h = thick_ref[c]
        thick_out[c] = h + gap / (h + 0.1)

    receive(8, ext, eargs, efargs)
    u, v, s1, s2, s3, strn, ca, cb = [ext[f] for f in range(8)]
    wide = (rows + 2 * HALO, 2 * cols)
    inner = slice(HALO, HALO + rows)
    g1 = g2 = cc = None
    for step in range(ITERS):
        ue = pltpu.roll(u, wide[1] - 1, axis=1) - pltpu.roll(u, 1, axis=1)
        vn = pltpu.roll(v, wide[0] - 1, axis=0) - pltpu.roll(v, 1, axis=0)
        un = pltpu.roll(u, wide[0] - 1, axis=0) - pltpu.roll(u, 1, axis=0)
        ve = pltpu.roll(v, wide[1] - 1, axis=1) - pltpu.roll(v, 1, axis=1)
        div = (ue + vn) * 0.5
        ten = (ue - vn) * 0.5
        she = (un + ve) * 0.5
        zeta = strn * lax.rsqrt(div * div + (ten * ten + she * she) * 0.25 + 0.01)
        s1 = s1 * (2.0 / 3.0) + (zeta * div - strn) * (1.0 / 3.0)
        s2 = s2 * (2.0 / 3.0) + zeta * ten * (1.0 / 12.0)
        s3 = s3 * (2.0 / 3.0) + zeta * she * (1.0 / 24.0)
        if step == 0:
            receive(2, lext, largs, lfargs)
            g1, g2 = lext[0], lext[1]
            grow = gy * rows - HALO + lax.broadcasted_iota(jnp.int32, wide, 0)
            grow = jnp.where(grow >= m * rows, 2 * m * rows - 1 - grow, grow)
            cc = ca * ((0.3 * 0.5 / (m * rows)) * (grow.astype(F32) + 0.5))
        part = (lambda x: x[inner, cols:]) if step == ITERS - 1 else (lambda x: x)

        def along(x):
            return part(pltpu.roll(x, wide[1] - 1, axis=1)) - part(pltpu.roll(x, 1, axis=1))

        def across(x):
            return part(pltpu.roll(x, wide[0] - 1, axis=0)) - part(pltpu.roll(x, 1, axis=0))

        fx = along(s1 + s2) * 0.25 + across(s3) * 0.5
        fy = along(s3) * 0.5 + across(s1 - s2) * 0.25
        u, v, a, b, c = part(u), part(v), part(ca), part(cb), part(cc)
        u, v = a * u + c * v + b * (fx + part(g1)), a * v - c * u + b * (fy + part(g2))

    vel_out[0] = u
    vel_out[1] = v
    str_out[0] = s1[inner, cols:]
    str_out[1] = s2[inner, cols:]
    str_out[2] = s3[inner, cols:]
    de = u - east
    dn = v - north
    melt = excess * jnp.sqrt(de * de + dn * dn + 0.01)
    land = land_ref[...].astype(F32)
    for c in range(thick_ref.shape[0]):
        thick_out[c] = land * jnp.maximum(thick_out[c] - melt, 0.0)

    each(n, lambda off: a2a(off).wait_send())
    wait_sends(eargs, efargs)
    wait_sends(largs, lfargs)


def emit(vel, stress, thick, vel_out, str_out, thick_out, sem):
    pairs = ((vel, vel_out), (stress, str_out), (thick, thick_out))
    copies = [pltpu.make_async_copy(src, dst, sem.at[i]) for i, (src, dst) in enumerate(pairs)]
    for copy in copies:
        copy.start()
    for copy in copies:
        copy.wait()


def body(n, m, *args):
    ocean, block_map, vel, stress, thick = args[:5]
    rows, cols = args[7].shape
    group = max(2, rows // n)
    nf, nl = 8, 2
    wide = (rows + 2 * HALO, 2 * cols)
    vmem = pl.BlockSpec(memory_space=pltpu.VMEM)
    hbm = pl.BlockSpec(memory_space=pltpu.MemorySpace.HBM)
    args = tuple(pltpu.with_memory_space_constraint(a, pltpu.MemorySpace.HBM) for a in (ocean, block_map.T) + args[2:])

    def bufs(k):
        return [
            pltpu.VMEM((k, 8, cols), F32),
            pltpu.VMEM((2, k, 8, cols), F32),
            pltpu.VMEM((2, k, 8, cols), F32),
            pltpu.VMEM((2, k, 8, cols), F32),
            pltpu.VMEM((2, 8, cols), F32),
            pltpu.VMEM((2, 2, 8, cols), F32),
        ]

    dma = pltpu.SemaphoreType.DMA
    shapes = (
        jax.ShapeDtypeStruct(vel.shape, F32),
        jax.ShapeDtypeStruct(stress.shape, F32),
        jax.ShapeDtypeStruct(thick.shape, F32),
    )
    results = pl.pallas_call(
        functools.partial(kernel, n, m),
        out_shape=shapes,
        in_specs=[hbm] * 11,
        out_specs=(vmem, vmem, vmem),
        scratch_shapes=[
            *[pltpu.VMEM(a.shape, a.dtype) for a in args[:10]],
            pltpu.SMEM(args[10].shape, jnp.int32),
            dma((11,)),
            pltpu.VMEM((3 * cols, 2 * cols), jnp.bfloat16),
            pltpu.VMEM((nf,) + wide, F32),
            pltpu.VMEM((nl,) + wide, F32),
            pltpu.VMEM((n, 5, group, cols), F32),
            pltpu.VMEM((n, 5, group, cols), F32),
            *bufs(nf),
            *bufs(nl),
            pltpu.VMEM((nf, 8, cols), F32),
            pltpu.VMEM((n, nf, 8, cols), F32),
            pltpu.VMEM((nl, 8, cols), F32),
            pltpu.VMEM((n, nl, 8, cols), F32),
            dma((n,)),
            dma((n,)),
            dma((8,)),
            dma((8,)),
            dma((8,)),
            dma((8,)),
            dma((n,)),
            dma((n,)),
            dma((n,)),
            dma((n,)),
        ],
        compiler_params=pltpu.CompilerParams(
            collective_id=0, has_side_effects=True, vmem_limit_bytes=24 * 1024 * 1024
        ),
    )(*args)
    return pl.pallas_call(
        emit,
        out_shape=shapes,
        in_specs=[vmem] * 3,
        out_specs=(hbm, hbm, hbm),
        scratch_shapes=[dma((3,))],
        compiler_params=pltpu.CompilerParams(vmem_limit_bytes=1024 * 1024),
    )(*results)


def solution(mesh):
    placed = (
        P("gy", None, "gx"),
        P("gy", "gx"),
        P(None, "gy", "gx"),
        P(None, "gy", "gx"),
        P(None, "gy", "gx"),
        P(None, "gy", "gx"),
        P(None, "gy", "gx"),
        P("gy", "gx"),
        P("gy", "gx"),
        P("gy", "gx"),
        P(),
    )
    return jax.shard_map(
        functools.partial(body, mesh.shape["gx"], mesh.shape["gy"]),
        mesh=mesh,
        in_specs=placed,
        out_specs=(P(None, "gy", "gx"), P(None, "gy", "gx"), P(None, "gy", "gx")),
        check_vma=False,
    )
```
